32 devices in a mesh: dp: 4 (over y, core), chan: 2 (over x), seq: 4 (over z).
Axes of the slice: x: 2, y: 2, z: 4, core: 2. Of those that a mesh axis runs over, the one named last changes fastest.
Arguments:
- query_input: bfloat16 [4, 512, 8192], P('dp', 'seq', 'chan'), may hold values from -6 to 6
- key_input: bfloat16 [4, 512, 8192], P('dp', 'seq', 'chan'), may hold values from -6 to 6
- value_input: bfloat16 [4, 512, 8192], P('dp', 'seq', 'chan'), may hold values from -6 to 6
- grad_output: bfloat16 [4, 512, 8192], P('dp', 'seq', 'chan'), may hold values from -6 to 6
- w_embed: float32 [32, 64], replicated, may hold values from -6 to 6
- w_filter: float32 [64, 8192], P(None, ('chan', 'seq')), may hold values from -0.1875 to 0.1875
- decay_rates: float32 [8192], P(('chan', 'seq')), may hold values from 0.1 to 30.72
Outputs:
- d_query: bfloat16 [4, 512, 8192], P('dp', 'seq', 'chan')
- d_key: bfloat16 [4, 512, 8192], P('dp', 'seq', 'chan')
- d_value: bfloat16 [4, 512, 8192], P('dp', 'seq', 'chan')
- grad_filter: float32 [64, 8192], P(None, ('chan', 'seq'))
- grad_rate: float32 [8192], P(('chan', 'seq'))
- grad_embed: float32 [32, 64], replicated
The draws below stay inside these ranges and needn't reach their ends.
All inputs are finite; a program needn't handle non-finite values.
Results may differ from the reference program's by a relative error of at most 0.0058.
Values may be sent and summed in bfloat16 or wider, within the bound.
A program may use at most 128 MiB of HBM per device.

```python
import math
import jax
import jax.numpy as jnp
from jax import lax

D = 8192
HID = 64
EMB = 32
LENGTH = 512
BATCH = 4


def shard_levels(key, shape, pieces, least, high):
    factor_of = 1.0
    for dim, parts in pieces:
        heights = jax.random.uniform(jax.random.fold_in(jax.random.fold_in(key, 6), dim), (parts,), jnp.float32, least / len(pieces), high / len(pieces))
        factor_of = factor_of * jnp.repeat(jnp.exp(heights), shape[dim] // parts).reshape((-1,) + (1,) * (len(shape) - 1 - dim))
    return factor_of


def bell_draw(key, shape, spread, reach, shards=(), held_as=jnp.bfloat16):
    gain = shard_levels(key, shape, shards, -0.22, 0.18) if shards else 1.0
    result = jax.random.normal(key, shape, jnp.float32) * spread * gain
    return jnp.minimum(jnp.maximum(result, -reach), reach).astype(held_as)


def setup_inputs(seed: int = 0) -> dict:
    arg_keys = jax.random.split(jax.random.key(seed), 8)
    return {
        "query_input": bell_draw(arg_keys[0], (BATCH, LENGTH, D), 1.0, 6.0, ((0, 4), (1, 4), (2, 2))),
        "key_input": bell_draw(arg_keys[1], (BATCH, LENGTH, D), 1.0, 6.0, ((0, 4), (1, 4), (2, 2))),
        "value_input": bell_draw(arg_keys[2], (BATCH, LENGTH, D), 1.0, 6.0, ((0, 4), (1, 4), (2, 2))),
        "grad_output": bell_draw(arg_keys[3], (BATCH, LENGTH, D), 1.0, 6.0, ((0, 4), (1, 4), (2, 2))),
        "w_embed": bell_draw(arg_keys[4], (EMB, HID), 1.0, 6.0, (), jnp.float32),
        "w_filter": bell_draw(arg_keys[5], (HID, D), (16 * HID) ** -0.5, 0.1875, ((1, 8),), jnp.float32),
        "decay_rates": jnp.clip(jnp.exp(math.log(30.72) - 5.727499 * jax.random.uniform(arg_keys[6], (D,), jnp.float32) ** shard_levels(arg_keys[6], (D,), ((0, 8),), -0.2, 0.2)), 0.1, 30.72),
    }


def embed_features(positions, count, length):
    bands = jnp.arange(count // 2, dtype=jnp.float32) + 0.5
    phase = positions[None, :] * bands[:, None] * (2.0 * math.pi / length)
    return jnp.concatenate([jnp.sin(phase), jnp.cos(phase)], axis=0)

def reference(query_input, key_input, value_input, grad_output, w_embed, w_filter, decay_rates):
    batch_count, length, width_total = query_input.shape
    fft_size = 2 * length
    positions = jnp.arange(length, dtype=jnp.float32)
    features = embed_features(positions, w_embed.shape[0], length)
    pre_act = jnp.dot(features.T, w_embed, precision=lax.Precision.HIGHEST)
    hidden = jnp.sin(pre_act)
    block_size = min(256, width_total)
    block_count = width_total // block_size
    loss_scale = 1.0 / math.sqrt(batch_count * length)
    time_scale = 1.0 / math.sqrt(length)

    def one_block(offset):

        def pick(array):
            return lax.dynamic_slice_in_dim(array, offset, block_size, 2).astype(jnp.float32)
        queries = pick(query_input)
        keys_full = pick(key_input)
        values_full = pick(value_input)
        grads_full = pick(grad_output)
        product = (keys_full * values_full).astype(jnp.bfloat16)
        upstream = (grads_full * queries).astype(jnp.bfloat16)
        product, upstream = lax.optimization_barrier((product, upstream))
        product = product.astype(jnp.float32)
        upstream = upstream.astype(jnp.float32)
        filter_block = lax.dynamic_slice_in_dim(w_filter, offset, block_size, 1)
        rate_block = lax.dynamic_slice_in_dim(decay_rates, offset, block_size, 0)
        window = jnp.exp(-rate_block[None, :] * positions[:, None] / length)
        filter_taps = jnp.dot(hidden, filter_block, precision=lax.Precision.HIGHEST) * window
        filter_spec = jnp.fft.rfft(filter_taps, n=fft_size, axis=0)
        input_spec = jnp.fft.rfft(product, n=fft_size, axis=1)
        grad_spec = jnp.fft.rfft(upstream, n=fft_size, axis=1)
        conv_out = jnp.fft.irfft(filter_spec[None] * input_spec, n=fft_size, axis=1)[:, :length]
        conv_grad = jnp.fft.irfft(jnp.conj(filter_spec)[None] * grad_spec, n=fft_size, axis=1)[:, :length]
        correlation = jnp.fft.irfft(jnp.conj(input_spec) * grad_spec, n=fft_size, axis=1)[:, :length]
        correlation = lax.optimization_barrier(jnp.sum(correlation, axis=0)) * loss_scale
        conv_out = lax.optimization_barrier(conv_out.astype(jnp.bfloat16)).astype(jnp.float32)
        conv_grad = lax.optimization_barrier(conv_grad.astype(jnp.bfloat16)).astype(jnp.float32)
        d_query = (grads_full * conv_out).astype(jnp.bfloat16)
        d_key = (conv_grad * values_full).astype(jnp.bfloat16)
        d_value = (conv_grad * keys_full).astype(jnp.bfloat16)
        weighted = correlation * window
        grad_filter = jnp.dot(hidden.T, weighted, precision=lax.Precision.HIGHEST) * time_scale
        grad_rate = -lax.optimization_barrier(jnp.sum(positions[:, None] / length * filter_taps * correlation, axis=0)) * time_scale
        hidden_grad = jnp.dot(weighted, filter_block.T, precision=lax.Precision.HIGHEST)
        return (d_query, d_key, d_value, grad_filter, grad_rate, hidden_grad)
    offsets = (jnp.arange(block_count) * block_size).astype(jnp.int32)
    d_query, d_key, d_value, grad_filter, grad_rate, hidden_grad = lax.map(one_block, offsets)

    def assemble(stacked):
        return jnp.transpose(stacked, (1, 2, 0, 3)).reshape(batch_count, length, width_total)
    grad_filter = jnp.transpose(grad_filter, (1, 0, 2)).reshape(w_filter.shape[0], width_total)
    grad_rate = grad_rate.reshape(width_total)
    hidden_sum = lax.optimization_barrier(jnp.sum(hidden_grad, axis=0))
    grad_embed = jnp.dot(features, hidden_sum * jnp.cos(pre_act), precision=lax.Precision.HIGHEST) * time_scale
    return (assemble(d_query), assemble(d_key), assemble(d_value), grad_filter, grad_rate, grad_embed)
```

```python
import functools
import math

import jax
import jax.numpy as jnp
import numpy as np
from jax import lax
from jax.experimental import pallas as pl
from jax.experimental.pallas import tpu as pltpu
from jax.sharding import PartitionSpec as P

HIGHEST = lax.Precision.HIGHEST
MESH = pl.DeviceIdType.MESH
NARROW = jnp.bfloat16
WIDE = jnp.float32


def embed_features(length, count):
    bands = np.arange(count // 2) + 0.5
    phase = np.arange(length)[None, :] * bands[:, None] * (2.0 * np.pi / length)
    return np.concatenate([np.sin(phase), np.cos(phase)], axis=0).astype(np.float32)


def dft_tables(length):
    turns = np.outer(2 * np.arange(length) + 1, np.arange(length)) % (4 * length)
    angles = turns * (2.0 * np.pi / (4 * length))
    forward = np.concatenate([np.cos(angles), np.sin(angles)], axis=0)
    half = length // 2
    by_half = np.stack([forward[:, :half], forward[:, half:]])
    return by_half.astype(NARROW)


def dot(a, b, dims=((1,), (0,)), precision=None):
    return lax.dot_general(a, b, (dims, ((), ())), preferred_element_type=WIDE, precision=precision)


def doubling_steps(size):
    return [1 << i for i in range(size.bit_length() - 1)]


def flip(index, bit):
    return index + bit - 2 * bit * (lax.rem(lax.div(index, bit), 2))


def kernel(sizes, tile, q_ref, k_ref, v_ref, g_ref, hidden_ref, hidden_t_ref, cos_ref, feat_ref,
           filter_ref, rate_ref, fwd_ref, dq_ref, dk_ref, dv_ref, grad_ref, embed_ref,
           inv_ref, src, a_buf, b_buf, out_buf, ret_buf, hg_buf, g_sum, g_got, e_sum, e_got,
           in_send, in_recv, ret_send, ret_recv, red_send, red_recv, emb_send, emb_recv):
    n, dpn, chn = sizes
    half = n // 2
    rows, width = q_ref.shape
    length = rows * n
    span = rows * half
    group = width // half
    tiles = group // tile
    hid = hidden_t_ref.shape[0]
    me = lax.axis_index("seq")
    dp = lax.axis_index("dp")
    ch = lax.axis_index("chan")
    up = lax.div(me, half)
    slot = lax.rem(me, half)

    barrier = pltpu.get_barrier_semaphore()
    greeted = 0
    for o in range(1, n):
        pl.semaphore_signal(barrier, inc=1, device_id=(dp, ch, lax.rem(me + o, n)), device_id_type=MESH)
        greeted += 1
    for bit in doubling_steps(dpn):
        pl.semaphore_signal(barrier, inc=1, device_id=(flip(dp, bit), ch, me), device_id_type=MESH)
        greeted += 1
    for bit in doubling_steps(chn):
        pl.semaphore_signal(barrier, inc=1, device_id=(dp, flip(ch, bit), me), device_id_type=MESH)
        greeted += 1
    pl.semaphore_wait(barrier, greeted)

    def col(owner, t):
        return pl.ds(pl.multiple_of(owner * group + t * tile, 128), tile)

    def tcol(t):
        return pl.ds(pl.multiple_of(t * tile, 128), tile)

    my_rows = pl.ds(pl.multiple_of(slot * rows, 16), rows)

    def in_copy(t, o, kind):
        owner = lax.rem(slot + o, half)
        dest = (dp, ch, (up if kind < 2 else 1 - up) * half + owner)
        source = src.at[0 if kind == 0 else 1, :, col(owner, t)]
        if kind == 1:
            target = b_buf.at[my_rows, tcol(t)]
        else:
            target = a_buf.at[up, my_rows, tcol(t)]
        return pltpu.make_async_remote_copy(
            src_ref=source, dst_ref=target, send_sem=in_send.at[t, o, kind],
            recv_sem=in_recv.at[t, o, kind], device_id=dest, device_id_type=MESH)

    def in_kinds(o):
        return (0, 1, 2) if o else (2,)

    def ret_copy(t, o, j):
        owner = lax.rem(slot + o, half)
        return pltpu.make_async_remote_copy(
            src_ref=out_buf.at[j, pl.ds(pl.multiple_of(owner * rows, 16), rows), tcol(t)],
            dst_ref=ret_buf.at[j, :, col(slot, t)],
            send_sem=ret_send.at[t, o, j], recv_sem=ret_recv.at[t, o, j],
            device_id=(dp, ch, up * half + owner), device_id_type=MESH)

    @pl.loop(0, tiles)
    def _(t):
        for o in list(range(1, half)) + [0]:
            owner = lax.rem(slot + o, half)
            c = col(owner, t)
            p = k_ref[:, c].astype(WIDE) * v_ref[:, c].astype(WIDE)
            u = g_ref[:, c].astype(WIDE) * q_ref[:, c].astype(WIDE)
            src[1 - up, :, c] = p.astype(NARROW)
            src[up, :, c] = u.astype(NARROW)
            for kind in in_kinds(o):
                in_copy(t, o, kind).start()
        c = col(slot, t)
        a_buf[up, my_rows, tcol(t)] = src[0, :, c]
        b_buf[my_rows, tcol(t)] = src[1, :, c]

    sign = (2 * up - 1).astype(WIDE)
    scale = 1.0 / (length * math.sqrt(dpn * length))
    time_scale = 1.0 / math.sqrt(length)
    hg_buf[...] = jnp.zeros_like(hg_buf)
    for i in (0, 1):
        inv_ref[i] = fwd_ref[i].T

    @pl.loop(0, tiles)
    def _(t):
        tc = tcol(t)
        positions = lax.broadcasted_iota(jnp.int32, (length, tile), 0).astype(WIDE) * (1.0 / length)
        window = jnp.exp(-rate_ref[:, tc] * positions)
        wf = filter_ref[:, tc]
        taps = dot(hidden_ref[...], wf) * window
        taps_n = taps.astype(NARROW)
        h = dot(fwd_ref[0], taps_n[:span]) + dot(fwd_ref[1], taps_n[span:])
        hc, hs = h[:length] * (1.0 / length), h[length:] * (sign / length)
        for o in range(half):
            for kind in in_kinds(o):
                in_copy(t, o, kind).wait_recv()
        b = dot(fwd_ref[up], b_buf[:, tc])
        mine = dot(fwd_ref[up], a_buf[up, :, tc])
        other = dot(fwd_ref[1 - up], a_buf[1 - up, :, tc])
        a = mine + other
        ac, as_ = a[:length], a[length:]
        bc, bs = b[:length], b[length:]

        def join(x, y):
            return jnp.concatenate([x.astype(NARROW), y.astype(NARROW)], axis=0)

        out_buf[0, :, tc] = dot(inv_ref[up], join(hc * ac - hs * as_, hc * as_ + hs * ac)).astype(NARROW)
        out_buf[1, :, tc] = dot(inv_ref[up], join(hc * bc + hs * bs, hc * bs - hs * bc)).astype(NARROW)
        for o in range(1, half):
            for j in (0, 1):
                ret_copy(t, o, j).start()
        for j in (0, 1):
            ret_buf[j, :, col(slot, t)] = out_buf[j, my_rows, tc]
        m = mine + 0.5 * other
        mc, ms = m[:length], m[length:]
        corr_n = join(mc * bc + ms * bs, (mc * bs - ms * bc) * sign)
        corr = jnp.concatenate([dot(inv_ref[0], corr_n), dot(inv_ref[1], corr_n)], axis=0) * scale
        weighted = (corr * window).astype(NARROW)
        g_sum[0, 0:hid, tc] = dot(hidden_t_ref[...], weighted) * time_scale
        rate = -jnp.sum(positions * taps * corr, axis=0, keepdims=True) * time_scale
        g_sum[0, hid:hid + 8, tc] = jnp.broadcast_to(rate, (8, tile))
        hg_buf[...] += dot(weighted, wf, ((1,), (1,)))

    e_sum[0] = dot(feat_ref[...], hg_buf[...] * cos_ref[...], precision=HIGHEST) * time_scale

    def exchange_embed(i, dest):
        copy = pltpu.make_async_remote_copy(
            src_ref=e_sum.at[i], dst_ref=e_got.at[i], send_sem=emb_send.at[i],
            recv_sem=emb_recv.at[i], device_id=dest, device_id_type=MESH)
        copy.start()
        return copy

    i = 0
    for bit in doubling_steps(dpn):
        dest = (flip(dp, bit), ch, me)
        copy = pltpu.make_async_remote_copy(
            src_ref=g_sum.at[i], dst_ref=g_got.at[i], send_sem=red_send.at[i],
            recv_sem=red_recv.at[i], device_id=dest, device_id_type=MESH)
        copy.start()
        exchange_embed(i, dest).wait()
        e_sum[i + 1] = e_sum[i] + e_got[i]
        copy.wait()
        g_sum[i + 1] = g_sum[i] + g_got[i]
        i += 1
    grad_ref[...] = g_sum[i]
    dests = [(dp, flip(ch, bit), me) for bit in doubling_steps(chn)]
    dests += [(dp, ch, flip(me, bit)) for bit in doubling_steps(n)]
    for dest in dests:
        exchange_embed(i, dest).wait()
        e_sum[i + 1] = e_sum[i] + e_got[i]
        i += 1
    embed_ref[...] = e_sum[i]

    @pl.loop(0, tiles)
    def _(t):
        for o in range(half):
            if o:
                for j in (0, 1):
                    ret_copy(t, o, j).wait()
            for kind in in_kinds(o):
                in_copy(t, o, kind).wait_send()
            c = col(lax.rem(slot - o + half, half), t)
            conv_out = ret_buf[1 - up, :, c].astype(WIDE)
            conv_grad = ret_buf[up, :, c].astype(WIDE)
            dq_ref[:, c] = (g_ref[:, c].astype(WIDE) * conv_out).astype(NARROW)
            dk_ref[:, c] = (conv_grad * v_ref[:, c].astype(WIDE)).astype(NARROW)
            dv_ref[:, c] = (conv_grad * k_ref[:, c].astype(WIDE)).astype(NARROW)


def per_device(query_input, key_input, value_input, grad_output, w_embed, w_filter, decay_rates):
    n, dpn, chn = lax.axis_size("seq"), lax.axis_size("dp"), lax.axis_size("chan")
    rows, width = query_input.shape[1:]
    length = rows * n
    half = n // 2
    group = width // half
    tile = min(group, 512)
    tiles = group // tile
    emb, hid = w_embed.shape

    features = jnp.asarray(embed_features(length, emb))
    pre = dot(features, w_embed, ((0,), (0,)), HIGHEST)
    hidden = jnp.sin(pre)
    forward = dft_tables(length)

    straight = [(2 * s, s) for s in range(half)] + [(2 * s + 1, s + half) for s in range(half)]
    crossed = [(2 * s + 1, s) for s in range(half)] + [(2 * s, s + half) for s in range(half)]
    upper = lax.axis_index("seq") >= half
    joined = jnp.concatenate([w_filter, decay_rates[None, :]], axis=0)
    first = lax.ppermute(joined, "seq", straight)
    second = lax.ppermute(joined, "seq", crossed)
    params = jnp.where(
        upper, jnp.concatenate([second, first], axis=1), jnp.concatenate([first, second], axis=1))

    vmem = pl.BlockSpec(memory_space=pltpu.VMEM)
    dma = pltpu.SemaphoreType.DMA
    dp_steps = len(doubling_steps(dpn))
    steps = dp_steps + len(doubling_steps(chn)) + len(doubling_steps(n))
    block = jax.ShapeDtypeStruct((rows, width), NARROW)
    out = pl.pallas_call(
        functools.partial(kernel, (n, dpn, chn), tile),
        out_shape=(block, block, block, jax.ShapeDtypeStruct((hid + 8, group), WIDE),
                   jax.ShapeDtypeStruct((emb, hid), WIDE)),
        in_specs=[vmem] * 11,
        out_specs=(vmem,) * 5,
        scratch_shapes=[
            pltpu.VMEM((2, half * rows, 2 * length), NARROW),
            pltpu.VMEM((2, rows, width), NARROW),
            pltpu.VMEM((2, half * rows, group), NARROW),
            pltpu.VMEM((half * rows, group), NARROW),
            pltpu.VMEM((2, half * rows, group), NARROW),
            pltpu.VMEM((2, rows, width), NARROW),
            pltpu.VMEM((length, hid), WIDE),
            pltpu.VMEM((dp_steps + 1, hid + 8, group), WIDE),
            pltpu.VMEM((dp_steps, hid + 8, group), WIDE),
            pltpu.VMEM((steps + 1, emb, hid), WIDE),
            pltpu.VMEM((steps, emb, hid), WIDE),
            dma((tiles, half, 3)), dma((tiles, half, 3)),
            dma((tiles, half, 2)), dma((tiles, half, 2)),
            dma((dp_steps,)), dma((dp_steps,)),
            dma((steps,)), dma((steps,)),
        ],
        compiler_params=pltpu.CompilerParams(
            collective_id=0, has_side_effects=True, vmem_limit_bytes=60 * 1024 * 1024),
        cost_estimate=pl.CostEstimate(flops=10**10, bytes_accessed=10**7, transcendentals=10**6),
    )(query_input[0], key_input[0], value_input[0], grad_output[0],
      hidden.astype(NARROW), hidden.T.astype(NARROW), jnp.cos(pre), features,
      params[:hid].astype(NARROW), params[hid:], forward)
    d_query, d_key, d_value, partial, grad_embed = out

    mine = group // 2
    left, right = partial[:hid + 1, :mine], partial[:hid + 1, mine:]
    back_straight = [(b, a) for a, b in straight]
    back_crossed = [(b, a) for a, b in crossed]
    total = lax.ppermute(jnp.where(upper, right, left), "seq", back_straight)
    total = total + lax.ppermute(jnp.where(upper, left, right), "seq", back_crossed)
    return (d_query[None], d_key[None], d_value[None], total[:hid], total[hid], grad_embed)


def solution(mesh):
    block = P("dp", "seq", "chan")
    in_specs = (block, block, block, block, P(), P(None, ("chan", "seq")), P(("chan", "seq")))
    out_specs = (block, block, block, P(None, ("chan", "seq")), P(("chan", "seq")), P())
    return jax.shard_map(
        per_device, mesh=mesh, in_specs=in_specs, out_specs=out_specs, check_vma=False
    )
```

```python
import functools
import math

import jax
import jax.numpy as jnp
import numpy as np
from jax import lax
from jax.experimental import pallas as pl
from jax.experimental.pallas import tpu as pltpu
from jax.sharding import PartitionSpec as P

HIGHEST = lax.Precision.HIGHEST
MESH = pl.DeviceIdType.MESH
NARROW = jnp.bfloat16
WIDE = jnp.float32


def embed_features(length, count):
    bands = np.arange(count // 2) + 0.5
    phase = np.arange(length)[None, :] * bands[:, None] * (2.0 * np.pi / length)
    return np.concatenate([np.sin(phase), np.cos(phase)], axis=0).astype(np.float32)


def dft_tables(length):
    turns = np.outer(2 * np.arange(length) + 1, np.arange(length)) % (4 * length)
    angles = turns * (2.0 * np.pi / (4 * length))
    forward = np.concatenate([np.cos(angles), np.sin(angles)], axis=0)
    half = length // 2
    by_half = np.stack([forward[:, :half], forward[:, half:]])
    return by_half.astype(NARROW)


def dot(a, b, dims=((1,), (0,)), precision=None):
    return lax.dot_general(a, b, (dims, ((), ())), preferred_element_type=WIDE, precision=precision)


def doubling_steps(size):
    return [1 << i for i in range(size.bit_length() - 1)]


def flip(index, bit):
    return index + bit - 2 * bit * (lax.rem(lax.div(index, bit), 2))


def kernel(sizes, tile, q_ref, k_ref, v_ref, g_ref, hidden_ref, hidden_t_ref, cos_ref, feat_ref,
           filter_ref, rate_ref, fwd_ref, conv_ref, grad_ref, embed_ref,
           inv_ref, src, a_buf, b_buf, out_buf, h_buf, taps_buf, win_buf, taps_n, corr_buf, weighted_n,
           mine_buf, other_buf, b_spec, join_1, join_2, join_3,
           filter_buf, rate_buf, hg_buf, g_sum, g_got, fin_src, fin_got, e_sum, e_got,
           in_send, in_recv, ret_send, ret_recv, own_sem, red_send, red_recv, emb_send, emb_recv,
           par_send, par_recv, rat_send, rat_recv, fin_send, fin_recv):
    n, dpn, chn = sizes
    half = n // 2
    rows, width = q_ref.shape
    length = rows * n
    span = rows * half
    group = width // half
    part = group // 2
    tiles = group // tile
    hid = hidden_t_ref.shape[0]
    me = lax.axis_index("seq")
    dp = lax.axis_index("dp")
    ch = lax.axis_index("chan")
    up = lax.div(me, half)
    slot = lax.rem(me, half)
    pair = lax.div(me, 2)
    parity = lax.rem(me, 2)

    barrier = pltpu.get_barrier_semaphore()
    greeted = 0
    for o in range(1, n):
        pl.semaphore_signal(barrier, inc=1, device_id=(dp, ch, lax.rem(me + o, n)), device_id_type=MESH)
        greeted += 1
    for bit in doubling_steps(dpn):
        pl.semaphore_signal(barrier, inc=1, device_id=(flip(dp, bit), ch, me), device_id_type=MESH)
        greeted += 1
    for bit in doubling_steps(chn):
        pl.semaphore_signal(barrier, inc=1, device_id=(dp, flip(ch, bit), me), device_id_type=MESH)
        greeted += 1
    pl.semaphore_wait(barrier, greeted)

    def col(owner, t):
        return pl.ds(pl.multiple_of(owner * group + t * tile, 128), tile)

    def tcol(t):
        return pl.ds(pl.multiple_of(t * tile, 128), tile)

    def block_rows(i, size, base=0):
        return pl.ds(pl.multiple_of(base + i * size, 16), size)

    my_rows = pl.ds(pl.multiple_of(slot * rows, 16), rows)

    def par_copies(j):
        dest = (dp, ch, pair + j * half)
        return [
            pltpu.make_async_remote_copy(
                src_ref=source, dst_ref=target.at[parity], send_sem=send.at[j],
                recv_sem=recv.at[parity], device_id=dest, device_id_type=MESH)
            for source, target, send, recv in (
                (filter_ref, filter_buf, par_send, par_recv), (rate_ref, rate_buf, rat_send, rat_recv))]

    def par_arrivals(e):
        return [
            pltpu.make_async_remote_copy(
                src_ref=source, dst_ref=target.at[e], send_sem=send.at[0],
                recv_sem=recv.at[e], device_id=(dp, ch, lax.rem(me + 1, n)), device_id_type=MESH)
            for source, target, send, recv in (
                (filter_ref, filter_buf, par_send, par_recv), (rate_ref, rate_buf, rat_send, rat_recv))]

    for j in (0, 1):
        @pl.when(pair + j * half != me)
        def _():
            for copy in par_copies(j):
                copy.start()

        @pl.when(pair + j * half == me)
        def _():
            filter_buf[parity] = filter_ref[...]
            rate_buf[parity] = rate_ref[...]

    def in_copy(t, o, kind):
        owner = lax.rem(slot + o, half)
        dest = (dp, ch, (up if kind < 2 else 1 - up) * half + owner)
        source = src.at[0 if kind == 0 else 1, :, col(owner, t)]
        if kind == 1:
            target = b_buf.at[my_rows, tcol(t)]
        else:
            target = a_buf.at[up, my_rows, tcol(t)]
        return pltpu.make_async_remote_copy(
            src_ref=source, dst_ref=target, send_sem=in_send.at[t, o, kind],
            recv_sem=in_recv.at[t, o, kind], device_id=dest, device_id_type=MESH)

    def in_kinds(o):
        return (0, 1, 2) if o else (2,)

    def ret_target(t, j):
        return conv_ref.at[1 - up if j == 0 else up, :, col(slot, t)]

    def ret_copy(t, o, j):
        owner = lax.rem(slot + o, half)
        return pltpu.make_async_remote_copy(
            src_ref=out_buf.at[j, pl.ds(pl.multiple_of(owner * rows, 16), rows), tcol(t)],
            dst_ref=ret_target(t, j),
            send_sem=ret_send.at[t, o, j], recv_sem=ret_recv.at[t, o, j],
            device_id=(dp, ch, up * half + owner), device_id_type=MESH)

    def own_copy(t, j):
        return pltpu.make_async_copy(out_buf.at[j, my_rows, tcol(t)], ret_target(t, j), own_sem.at[t, j])

    @pl.loop(0, tiles)
    def _(t):
        for o in list(range(1, half)) + [0]:
            owner = lax.rem(slot + o, half)
            c = col(owner, t)
            p = k_ref[:, c].astype(WIDE) * v_ref[:, c].astype(WIDE)
            u = g_ref[:, c].astype(WIDE) * q_ref[:, c].astype(WIDE)
            src[1 - up, :, c] = p.astype(NARROW)
            src[up, :, c] = u.astype(NARROW)
            for kind in in_kinds(o):
                in_copy(t, o, kind).start()
        c = col(slot, t)
        a_buf[up, my_rows, tcol(t)] = src[0, :, c]
        b_buf[my_rows, tcol(t)] = src[1, :, c]

    sign = (2 * up - 1).astype(WIDE)
    scale = 1.0 / (length * math.sqrt(dpn * length))
    time_scale = 1.0 / math.sqrt(length)
    hg_buf[...] = jnp.zeros_like(hg_buf)
    for i in (0, 1):
        inv_ref[i] = fwd_ref[i].T
    for e in (0, 1):
        @pl.when(2 * slot + e != me)
        def _():
            for copy in par_arrivals(e):
                copy.wait_recv()

    def pick(ref, t):
        if tile <= part:
            per = part // tile
            return ref[lax.div(t, per), :, tcol(lax.rem(t, per))]
        return jnp.concatenate([ref[0], ref[1]], axis=1)

    step = 32

    def places(i):
        at = lax.broadcasted_iota(jnp.int32, (step, tile), 0) + i * step
        return at.astype(WIDE) * (1.0 / length)

    @pl.loop(0, tiles)
    def _(t):
        tc = tcol(t)
        corr_buf[...] = dot(hidden_ref[...], pick(filter_buf, t))
        rate = pick(rate_buf, t)[0:1]

        @pl.loop(0, length // step)
        def _(i):
            r = block_rows(i, step)
            window = jnp.exp(-rate * places(i))
            taps = corr_buf[r, :] * window
            win_buf[r, tc] = window
            taps_buf[r, tc] = taps
            taps_n[r, :] = (taps * (1.0 / length)).astype(NARROW)

        h_buf[:, tc] = dot(fwd_ref[0], taps_n[:span]) + dot(fwd_ref[1], taps_n[span:])

    @pl.loop(0, tiles)
    def _(t):
        tc = tcol(t)
        for o in range(half):
            for kind in in_kinds(o):
                in_copy(t, o, kind).wait_recv()
        b_spec[...] = dot(fwd_ref[up], b_buf[:, tc])
        mine_buf[...] = dot(fwd_ref[up], a_buf[up, :, tc])
        other_buf[...] = dot(fwd_ref[1 - up], a_buf[1 - up, :, tc])

        @pl.loop(0, length // step)
        def _(i):
            c, s = block_rows(i, step), block_rows(i, step, length)
            hc, hs = h_buf[c, tc], h_buf[s, tc] * sign
            bc, bs = b_spec[c, :], b_spec[s, :]
            mc, ms = mine_buf[c, :], mine_buf[s, :]
            oc, os = other_buf[c, :], other_buf[s, :]
            ac, as_ = mc + oc, ms + os
            join_1[c, :] = (hc * ac - hs * as_).astype(NARROW)
            join_1[s, :] = (hc * as_ + hs * ac).astype(NARROW)
            join_2[c, :] = (hc * bc + hs * bs).astype(NARROW)
            join_2[s, :] = (hc * bs - hs * bc).astype(NARROW)
            mc, ms = mc + 0.5 * oc, ms + 0.5 * os
            join_3[c, :] = (mc * bc + ms * bs).astype(NARROW)
            join_3[s, :] = ((mc * bs - ms * bc) * sign).astype(NARROW)

        out_buf[0, :, tc] = dot(inv_ref[up], join_1[...]).astype(NARROW)
        out_buf[1, :, tc] = dot(inv_ref[up], join_2[...]).astype(NARROW)
        for o in range(1, half):
            for j in (0, 1):
                ret_copy(t, o, j).start()
        for j in (0, 1):
            own_copy(t, j).start()
        for i in (0, 1):
            corr_buf[i * span:(i + 1) * span] = dot(inv_ref[i], join_3[...])

        def finish(i, rate):
            r = block_rows(i, step)
            corr = corr_buf[r, :] * scale
            weighted_n[r, :] = (corr * win_buf[r, tc]).astype(NARROW)
            return rate + jnp.sum(places(i) * taps_buf[r, tc] * corr, axis=0, keepdims=True)

        rate = lax.fori_loop(0, length // step, finish, jnp.zeros((1, tile), WIDE))
        g_sum[0, 0:hid, tc] = dot(hidden_t_ref[...], weighted_n[...]) * time_scale
        g_sum[0, hid:hid + 8, tc] = jnp.broadcast_to(rate * -time_scale, (8, tile))
        hg_buf[...] += dot(weighted_n[...], pick(filter_buf, t), ((1,), (1,)))

    def exchange_embed(i, dest):
        copy = pltpu.make_async_remote_copy(
            src_ref=e_sum.at[i], dst_ref=e_got.at[i], send_sem=emb_send.at[i],
            recv_sem=emb_recv.at[i], device_id=dest, device_id_type=MESH)
        copy.start()
        return copy

    i = 0
    for bit in doubling_steps(dpn):
        dest = (flip(dp, bit), ch, me)
        copy = pltpu.make_async_remote_copy(
            src_ref=g_sum.at[i], dst_ref=g_got.at[i], send_sem=red_send.at[i],
            recv_sem=red_recv.at[i], device_id=dest, device_id_type=MESH)
        copy.start()
        if i == 0:
            e_sum[0] = dot(feat_ref[...], hg_buf[...] * cos_ref[...], precision=HIGHEST) * time_scale
        exchange_embed(i, dest).wait()
        e_sum[i + 1] = e_sum[i] + e_got[i]
        copy.wait()
        g_sum[i + 1] = g_sum[i] + g_got[i]
        i += 1

    for e in (0, 1):
        fin_src[e] = g_sum[i, :, e * part:(e + 1) * part]

    def fin_copy(e):
        return pltpu.make_async_remote_copy(
            src_ref=fin_src.at[e], dst_ref=fin_got.at[up], send_sem=fin_send.at[e],
            recv_sem=fin_recv.at[up], device_id=(dp, ch, 2 * slot + e), device_id_type=MESH)

    def fin_arrival(j):
        return pltpu.make_async_remote_copy(
            src_ref=fin_src.at[0], dst_ref=fin_got.at[j], send_sem=fin_send.at[0],
            recv_sem=fin_recv.at[j], device_id=(dp, ch, lax.rem(me + 1, n)), device_id_type=MESH)

    for e in (0, 1):
        @pl.when(2 * slot + e != me)
        def _():
            fin_copy(e).start()

        @pl.when(2 * slot + e == me)
        def _():
            fin_got[up] = fin_src[e]

    dests = [(dp, flip(ch, bit), me) for bit in doubling_steps(chn)]
    dests += [(dp, ch, flip(me, bit)) for bit in doubling_steps(n)]
    for dest in dests:
        exchange_embed(i, dest).wait()
        e_sum[i + 1] = e_sum[i] + e_got[i]
        i += 1
    embed_ref[...] = e_sum[i]

    for j in (0, 1):
        @pl.when(pair + j * half != me)
        def _():
            fin_arrival(j).wait_recv()
            for copy in par_copies(j):
                copy.wait_send()
    for e in (0, 1):
        @pl.when(2 * slot + e != me)
        def _():
            fin_copy(e).wait_send()
    grad_ref[...] = fin_got[0] + fin_got[1]

    @pl.loop(0, tiles)
    def _(t):
        for o in range(half):
            for j in (0, 1):
                if o:
                    ret_copy(t, o, j).wait()
                else:
                    own_copy(t, j).wait()
            for kind in in_kinds(o):
                in_copy(t, o, kind).wait_send()


def per_device(query_input, key_input, value_input, grad_output, w_embed, w_filter, decay_rates):
    n, dpn, chn = lax.axis_size("seq"), lax.axis_size("dp"), lax.axis_size("chan")
    rows, width = query_input.shape[1:]
    length = rows * n
    half = n // 2
    span = half * rows
    group = width // half
    part = group // 2
    tile = min(group, 256)
    tiles = group // tile
    emb, hid = w_embed.shape

    features = jnp.asarray(embed_features(length, emb))
    pre = dot(features, w_embed, ((0,), (0,)), HIGHEST)
    hidden = jnp.sin(pre)
    forward = dft_tables(length)

    vmem = pl.BlockSpec(memory_space=pltpu.VMEM)
    dma = pltpu.SemaphoreType.DMA
    dp_steps = len(doubling_steps(dpn))
    steps = dp_steps + len(doubling_steps(chn)) + len(doubling_steps(n))
    conv, partial, grad_embed = pl.pallas_call(
        functools.partial(kernel, (n, dpn, chn), tile),
        out_shape=(jax.ShapeDtypeStruct((2, rows, width), NARROW),
                   jax.ShapeDtypeStruct((hid + 8, part), WIDE),
                   jax.ShapeDtypeStruct((emb, hid), WIDE)),
        in_specs=[vmem] * 11,
        out_specs=(pl.BlockSpec(memory_space=pl.ANY), vmem, vmem),
        scratch_shapes=[
            pltpu.VMEM((2, span, 2 * length), NARROW),
            pltpu.VMEM((2, rows, width), NARROW),
            pltpu.VMEM((2, span, group), NARROW),
            pltpu.VMEM((span, group), NARROW),
            pltpu.VMEM((2, span, group), NARROW),
            pltpu.VMEM((2 * length, group), WIDE),
            pltpu.VMEM((length, group), WIDE),
            pltpu.VMEM((length, group), WIDE),
            pltpu.VMEM((length, tile), NARROW),
            pltpu.VMEM((length, tile), WIDE),
            pltpu.VMEM((length, tile), NARROW),
            pltpu.VMEM((2 * length, tile), WIDE),
            pltpu.VMEM((2 * length, tile), WIDE),
            pltpu.VMEM((2 * length, tile), WIDE),
            pltpu.VMEM((2 * length, tile), NARROW),
            pltpu.VMEM((2 * length, tile), NARROW),
            pltpu.VMEM((2 * length, tile), NARROW),
            pltpu.VMEM((2, hid, part), NARROW),
            pltpu.VMEM((2, 8, part), WIDE),
            pltpu.VMEM((length, hid), WIDE),
            pltpu.VMEM((dp_steps + 1, hid + 8, group), WIDE),
            pltpu.VMEM((dp_steps, hid + 8, group), WIDE),
            pltpu.VMEM((2, hid + 8, part), WIDE),
            pltpu.VMEM((2, hid + 8, part), WIDE),
            pltpu.VMEM((steps + 1, emb, hid), WIDE),
            pltpu.VMEM((steps, emb, hid), WIDE),
            dma((tiles, half, 3)), dma((tiles, half, 3)),
            dma((tiles, half, 2)), dma((tiles, half, 2)), dma((tiles, 2)),
            dma((dp_steps,)), dma((dp_steps,)),
            dma((steps,)), dma((steps,)),
            dma((2,)), dma((2,)), dma((2,)), dma((2,)), dma((2,)), dma((2,)),
        ],
        compiler_params=pltpu.CompilerParams(
            collective_id=0, has_side_effects=True, vmem_limit_bytes=60 * 1024 * 1024),
        cost_estimate=pl.CostEstimate(flops=10**10, bytes_accessed=10**7, transcendentals=10**6),
    )(query_input[0], key_input[0], value_input[0], grad_output[0],
      hidden.astype(NARROW), hidden.T.astype(NARROW), jnp.cos(pre), features,
      w_filter.astype(NARROW), jnp.broadcast_to(decay_rates[None, :], (8, part)), forward)

    conv_out, conv_grad = conv[0:1].astype(WIDE), conv[1:2].astype(WIDE)
    d_query = (grad_output.astype(WIDE) * conv_out).astype(NARROW)
    d_key = (conv_grad * value_input.astype(WIDE)).astype(NARROW)
    d_value = (conv_grad * key_input.astype(WIDE)).astype(NARROW)
    return (d_query, d_key, d_value, partial[:hid], partial[hid], grad_embed)


def solution(mesh):
    block = P("dp", "seq", "chan")
    in_specs = (block, block, block, block, P(), P(None, ("chan", "seq")), P(("chan", "seq")))
    out_specs = (block, block, block, P(None, ("chan", "seq")), P(("chan", "seq")), P())
    return jax.shard_map(
        per_device, mesh=mesh, in_specs=in_specs, out_specs=out_specs, check_vma=False
    )
```

```python
import functools
import math

import jax
import jax.numpy as jnp
import numpy as np
from jax import lax
from jax.experimental import pallas as pl
from jax.experimental.pallas import tpu as pltpu
from jax.sharding import PartitionSpec as P

HIGHEST = lax.Precision.HIGHEST
MESH = pl.DeviceIdType.MESH
NARROW = jnp.bfloat16
WIDE = jnp.float32


def embed_features(length, count):
    bands = np.arange(count // 2) + 0.5
    phase = np.arange(length)[None, :] * bands[:, None] * (2.0 * np.pi / length)
    return np.concatenate([np.sin(phase), np.cos(phase)], axis=0).astype(np.float32)


def dft_tables(length):
    turns = np.outer(2 * np.arange(length) + 1, np.arange(length)) % (4 * length)
    angles = turns * (2.0 * np.pi / (4 * length))
    forward = np.concatenate([np.cos(angles), np.sin(angles)], axis=0)
    half = length // 2
    by_half = np.stack([forward[:, :half], forward[:, half:]])
    return by_half.astype(NARROW)


def dot(a, b, dims=((1,), (0,)), precision=None):
    return lax.dot_general(a, b, (dims, ((), ())), preferred_element_type=WIDE, precision=precision)


def doubling_steps(size):
    return [1 << i for i in range(size.bit_length() - 1)]


def flip(index, bit):
    return index + bit - 2 * bit * (lax.rem(lax.div(index, bit), 2))


def kernel(sizes, tile, q_ref, k_ref, v_ref, g_ref, embed_in, feat_ref, filter_in, rate_in, fwd_ref,
           conv_ref, grad_ref, grate_ref, embed_ref,
           filter_ref, rate_ref, hidden_ref, hidden_t_ref, cos_ref, gs_src, gs_got, red_src, fin_all,
           inv_ref, src, a_buf, b_buf, out_buf, h_buf, taps_buf, win_buf, taps_n, corr_buf, weighted_n,
           mine_buf, other_buf, b_spec, join_1, join_2, join_3,
           filter_buf, rate_buf, hg_buf, g_sum, g_got, fin_src, fin_got, e_sum, e_got,
           in_send, in_recv, ret_send, ret_recv, own_sem, red_send, red_recv, emb_send, emb_recv,
           par_send, par_recv, rat_send, rat_recv, fin_send, fin_recv,
           gs_send, gs_recv, all_send, all_recv):
    n, dpn, chn = sizes
    half = n // 2
    rows, width = q_ref.shape
    length = rows * n
    span = rows * half
    group = width // half
    part = group // 2
    tiles = group // tile
    hid = hidden_t_ref.shape[0]
    stream = tiles % (2 * dpn) == 0
    me = lax.axis_index("seq")
    dp = lax.axis_index("dp")
    ch = lax.axis_index("chan")
    up = lax.div(me, half)
    slot = lax.rem(me, half)
    pair = lax.div(me, 2)
    parity = lax.rem(me, 2)

    barrier = pltpu.get_barrier_semaphore()
    greeted = 0
    for o in range(1, n):
        pl.semaphore_signal(barrier, inc=1, device_id=(dp, ch, lax.rem(me + o, n)), device_id_type=MESH)
        greeted += 1
    for o in range(1, dpn):
        for other in ([lax.rem(me + d, n) for d in range(n)] if stream else [me]):
            pl.semaphore_signal(barrier, inc=1, device_id=(lax.rem(dp + o, dpn), ch, other), device_id_type=MESH)
            greeted += 1
    for o in range(1, chn):
        pl.semaphore_signal(barrier, inc=1, device_id=(dp, lax.rem(ch + o, chn), me), device_id_type=MESH)
        greeted += 1
    pl.semaphore_wait(barrier, greeted)

    def col(owner, t):
        return pl.ds(pl.multiple_of(owner * group + t * tile, 128), tile)

    def tcol(t):
        return pl.ds(pl.multiple_of(t * tile, 128), tile)

    def block_rows(i, size, base=0):
        return pl.ds(pl.multiple_of(base + i * size, 16), size)

    my_rows = pl.ds(pl.multiple_of(slot * rows, 16), rows)

    def par_copies(j):
        dest = (dp, ch, pair + j * half)
        return [
            pltpu.make_async_remote_copy(
                src_ref=source, dst_ref=target.at[parity], send_sem=send.at[j],
                recv_sem=recv.at[parity], device_id=dest, device_id_type=MESH)
            for source, target, send, recv in (
                (filter_ref, filter_buf, par_send, par_recv), (rate_ref, rate_buf, rat_send, rat_recv))]

    def par_arrivals(e):
        return [
            pltpu.make_async_remote_copy(
                src_ref=source, dst_ref=target.at[e], send_sem=send.at[0],
                recv_sem=recv.at[e], device_id=(dp, ch, lax.rem(me + 1, n)), device_id_type=MESH)
            for source, target, send, recv in (
                (filter_ref, filter_buf, par_send, par_recv), (rate_ref, rate_buf, rat_send, rat_recv))]

    filter_ref[...] = filter_in[...].astype(NARROW)
    rate_ref[...] = jnp.broadcast_to(rate_in[...], rate_ref.shape)
    for j in (0, 1):
        @pl.when(pair + j * half != me)
        def _():
            for copy in par_copies(j):
                copy.start()

        @pl.when(pair + j * half == me)
        def _():
            filter_buf[parity] = filter_ref[...]
            rate_buf[parity] = rate_ref[...]

    def in_copy(t, o, kind):
        owner = lax.rem(slot + o, half)
        dest = (dp, ch, (up if kind < 2 else 1 - up) * half + owner)
        source = src.at[0 if kind == 0 else 1, :, col(owner, t)]
        if kind == 1:
            target = b_buf.at[my_rows, tcol(t)]
        else:
            target = a_buf.at[up, my_rows, tcol(t)]
        return pltpu.make_async_remote_copy(
            src_ref=source, dst_ref=target, send_sem=in_send.at[t, o, kind],
            recv_sem=in_recv.at[t, o, kind], device_id=dest, device_id_type=MESH)

    def in_kinds(o):
        return (0, 1, 2) if o else (2,)

    def ret_target(t, j):
        return conv_ref.at[1 - up if j == 0 else up, :, col(slot, t)]

    def ret_copy(t, o, j):
        owner = lax.rem(slot + o, half)
        return pltpu.make_async_remote_copy(
            src_ref=out_buf.at[j, pl.ds(pl.multiple_of(owner * rows, 16), rows), tcol(t)],
            dst_ref=ret_target(t, j),
            send_sem=ret_send.at[t, o, j], recv_sem=ret_recv.at[t, o, j],
            device_id=(dp, ch, up * half + owner), device_id_type=MESH)

    def own_copy(t, j):
        return pltpu.make_async_copy(out_buf.at[j, my_rows, tcol(t)], ret_target(t, j), own_sem.at[t, j])

    @pl.loop(0, tiles)
    def _(t):
        for o in list(range(1, half)) + [0]:
            owner = lax.rem(slot + o, half)
            c = col(owner, t)
            p = k_ref[:, c].astype(WIDE) * v_ref[:, c].astype(WIDE)
            u = g_ref[:, c].astype(WIDE) * q_ref[:, c].astype(WIDE)
            src[1 - up, :, c] = p.astype(NARROW)
            src[up, :, c] = u.astype(NARROW)
            for kind in in_kinds(o):
                in_copy(t, o, kind).start()
        c = col(slot, t)
        a_buf[up, my_rows, tcol(t)] = src[0, :, c]
        b_buf[my_rows, tcol(t)] = src[1, :, c]

    each = max(1, tiles // (2 * dpn))

    def gs_dest(t):
        return lax.div(lax.rem(t, tiles // 2), each), ch, 2 * slot + lax.div(t, tiles // 2)

    def gs_place(t):
        return lax.rem(lax.rem(t, tiles // 2), each)

    def gs_copy(t):
        return pltpu.make_async_remote_copy(
            src_ref=gs_src.at[t], dst_ref=gs_got.at[gs_place(t), 2 * dp + up], send_sem=gs_send.at[t],
            recv_sem=gs_recv.at[gs_place(t), 2 * dp + up], device_id=gs_dest(t), device_id_type=MESH)

    def gs_arrival(i, c):
        return pltpu.make_async_remote_copy(
            src_ref=gs_src.at[0], dst_ref=gs_got.at[i, c], send_sem=gs_send.at[0],
            recv_sem=gs_recv.at[i, c], device_id=(dp, ch, lax.rem(me + 1, n)), device_id_type=MESH)

    def all_copy(i, o):
        return pltpu.make_async_remote_copy(
            src_ref=red_src.at[i], dst_ref=fin_all.at[:, tcol(dp * each + i)], send_sem=all_send.at[i, o],
            recv_sem=all_recv.at[i, o], device_id=(lax.rem(dp + o, dpn), ch, me), device_id_type=MESH)

    sign = (2 * up - 1).astype(WIDE)
    scale = 1.0 / (length * math.sqrt(dpn * length))
    time_scale = 1.0 / math.sqrt(length)
    hg_buf[...] = jnp.zeros_like(hg_buf)
    for i in (0, 1):
        inv_ref[i] = fwd_ref[i].T
    pre_t = dot(embed_in[...], feat_ref[...], ((0,), (0,)), HIGHEST)
    hidden_t = jnp.sin(pre_t)
    hidden_t_ref[...] = hidden_t.astype(NARROW)
    hidden_ref[...] = hidden_t.T.astype(NARROW)
    cos_ref[...] = jnp.cos(pre_t).T
    for e in (0, 1):
        @pl.when(2 * slot + e != me)
        def _():
            for copy in par_arrivals(e):
                copy.wait_recv()

    def pick(ref, t):
        if tile <= part:
            per = part // tile
            return ref[lax.div(t, per), :, tcol(lax.rem(t, per))]
        return jnp.concatenate([ref[0], ref[1]], axis=1)

    step = 32

    def places(i):
        at = lax.broadcasted_iota(jnp.int32, (step, tile), 0) + i * step
        return at.astype(WIDE) * (1.0 / length)

    @pl.loop(0, tiles)
    def _(t):
        tc = tcol(t)
        corr_buf[...] = dot(hidden_ref[...], pick(filter_buf, t))
        rate = pick(rate_buf, t)[0:1]

        @pl.loop(0, length // step)
        def _(i):
            r = block_rows(i, step)
            window = jnp.exp(-rate * places(i))
            taps = corr_buf[r, :] * window
            win_buf[r, tc] = window
            taps_buf[r, tc] = taps
            taps_n[r, :] = (taps * (1.0 / length)).astype(NARROW)

        h_buf[:, tc] = dot(fwd_ref[0], taps_n[:span]) + dot(fwd_ref[1], taps_n[span:])

    @pl.loop(0, tiles)
    def _(t):
        tc = tcol(t)
        for o in range(half):
            for kind in in_kinds(o):
                in_copy(t, o, kind).wait_recv()
        b_spec[...] = dot(fwd_ref[up], b_buf[:, tc])
        mine_buf[...] = dot(fwd_ref[up], a_buf[up, :, tc])
        other_buf[...] = dot(fwd_ref[1 - up], a_buf[1 - up, :, tc])

        @pl.loop(0, length // step)
        def _(i):
            c, s = block_rows(i, step), block_rows(i, step, length)
            hc, hs = h_buf[c, tc], h_buf[s, tc] * sign
            bc, bs = b_spec[c, :], b_spec[s, :]
            mc, ms = mine_buf[c, :], mine_buf[s, :]
            oc, os = other_buf[c, :], other_buf[s, :]
            ac, as_ = mc + oc, ms + os
            join_1[c, :] = (hc * ac - hs * as_).astype(NARROW)
            join_1[s, :] = (hc * as_ + hs * ac).astype(NARROW)
            join_2[c, :] = (hc * bc + hs * bs).astype(NARROW)
            join_2[s, :] = (hc * bs - hs * bc).astype(NARROW)
            mc, ms = mc + 0.5 * oc, ms + 0.5 * os
            join_3[c, :] = (mc * bc + ms * bs).astype(NARROW)
            join_3[s, :] = ((mc * bs - ms * bc) * sign).astype(NARROW)

        out_buf[0, :, tc] = dot(inv_ref[up], join_1[...]).astype(NARROW)
        out_buf[1, :, tc] = dot(inv_ref[up], join_2[...]).astype(NARROW)
        for o in range(1, half):
            for j in (0, 1):
                ret_copy(t, o, j).start()
        for j in (0, 1):
            own_copy(t, j).start()
        for i in (0, 1):
            corr_buf[i * span:(i + 1) * span] = dot(inv_ref[i], join_3[...])

        def finish(i, rate):
            r = block_rows(i, step)
            corr = corr_buf[r, :] * scale
            weighted_n[r, :] = (corr * win_buf[r, tc]).astype(NARROW)
            return rate + jnp.sum(places(i) * taps_buf[r, tc] * corr, axis=0, keepdims=True)

        rate = lax.fori_loop(0, length // step, finish, jnp.zeros((1, tile), WIDE))
        grad = dot(hidden_t_ref[...], weighted_n[...]) * time_scale
        rate = rate * -time_scale
        if stream:
            gs_src[t, 0:hid] = grad.astype(NARROW)
            gs_src[t, hid:hid + 16] = jnp.broadcast_to(rate, (16, tile)).astype(NARROW)
            mine = jnp.logical_and(gs_dest(t)[0] == dp, gs_dest(t)[2] == me)

            @pl.when(jnp.logical_not(mine))
            def _():
                gs_copy(t).start()

            @pl.when(mine)
            def _():
                gs_got[gs_place(t), 2 * dp + up] = gs_src[t]
        else:
            g_sum[0, 0:hid, tc] = grad
            g_sum[0, hid:hid + 8, tc] = jnp.broadcast_to(rate, (8, tile))
        hg_buf[...] += dot(weighted_n[...], pick(filter_buf, t), ((1,), (1,)))

    e_sum[0] = dot(feat_ref[...], hg_buf[...] * cos_ref[...], precision=HIGHEST) * time_scale

    def embed_round(axis, base, size, index, dest):
        def copy(o):
            return pltpu.make_async_remote_copy(
                src_ref=e_sum.at[axis], dst_ref=e_got.at[base + index], send_sem=emb_send.at[base + o],
                recv_sem=emb_recv.at[base + o], device_id=dest(lax.rem(index + o, size)), device_id_type=MESH)

        e_got[base + index] = e_sum[axis]
        for o in range(1, size):
            copy(o).start()
        for o in range(1, size):
            copy(o).wait()
        total = e_got[base]
        for o in range(1, size):
            total = total + e_got[base + o]
        e_sum[axis + 1] = total

    embed_round(0, 0, dpn, dp, lambda at: (at, ch, me))
    embed_round(1, dpn, chn, ch, lambda at: (dp, at, me))

    if stream:
        for i in range(each):
            total = jnp.zeros((hid + 8, tile), WIDE)
            for c in range(2 * dpn):
                mine = jnp.logical_and(dp == c // 2, (c % 2) * half + pair == me)

                @pl.when(jnp.logical_not(mine))
                def _():
                    gs_arrival(i, c).wait_recv()

                total = total + gs_got[i, c].astype(WIDE)[:hid + 8]
            red_src[i] = total
            for o in range(1, dpn):
                all_copy(i, o).start()
            fin_all[:, tcol(dp * each + i)] = total

    i = 0
    for bit in ([] if stream else doubling_steps(dpn)):
        copy = pltpu.make_async_remote_copy(
            src_ref=g_sum.at[i], dst_ref=g_got.at[i], send_sem=red_send.at[i],
            recv_sem=red_recv.at[i], device_id=(flip(dp, bit), ch, me), device_id_type=MESH)
        copy.start()
        copy.wait()
        g_sum[i + 1] = g_sum[i] + g_got[i]
        i += 1

    owners = () if stream else (0, 1)
    for e in owners:
        fin_src[e] = g_sum[i, :, e * part:(e + 1) * part]

    def fin_copy(e):
        return pltpu.make_async_remote_copy(
            src_ref=fin_src.at[e], dst_ref=fin_got.at[up], send_sem=fin_send.at[e],
            recv_sem=fin_recv.at[up], device_id=(dp, ch, 2 * slot + e), device_id_type=MESH)

    def fin_arrival(j):
        return pltpu.make_async_remote_copy(
            src_ref=fin_src.at[0], dst_ref=fin_got.at[j], send_sem=fin_send.at[0],
            recv_sem=fin_recv.at[j], device_id=(dp, ch, lax.rem(me + 1, n)), device_id_type=MESH)

    for e in owners:
        @pl.when(2 * slot + e != me)
        def _():
            fin_copy(e).start()

        @pl.when(2 * slot + e == me)
        def _():
            fin_got[up] = fin_src[e]

    embed_round(2, dpn + chn, n, me, lambda at: (dp, ch, at))
    embed_ref[...] = e_sum[3]

    for j in (0, 1):
        @pl.when(pair + j * half != me)
        def _():
            for copy in par_copies(j):
                copy.wait_send()
    for j in owners:
        @pl.when(pair + j * half != me)
        def _():
            fin_arrival(j).wait_recv()
    for e in owners:
        @pl.when(2 * slot + e != me)
        def _():
            fin_copy(e).wait_send()
    if stream:
        for i in range(each):
            for o in range(1, dpn):
                all_copy(i, o).wait()
    else:
        fin_all[...] = fin_got[0] + fin_got[1]
    grad_ref[...] = fin_all[0:hid]
    grate_ref[...] = fin_all[hid:hid + 8]

    @pl.loop(0, tiles)
    def _(t):
        for o in range(half):
            for j in (0, 1):
                if o:
                    ret_copy(t, o, j).wait()
                else:
                    own_copy(t, j).wait()
            for kind in in_kinds(o):
                in_copy(t, o, kind).wait_send()
        if stream:
            @pl.when(jnp.logical_not(jnp.logical_and(gs_dest(t)[0] == dp, gs_dest(t)[2] == me)))
            def _():
                gs_copy(t).wait_send()


def per_device(query_input, key_input, value_input, grad_output, w_embed, w_filter, decay_rates):
    n, dpn, chn = lax.axis_size("seq"), lax.axis_size("dp"), lax.axis_size("chan")
    rows, width = query_input.shape[1:]
    length = rows * n
    half = n // 2
    span = half * rows
    group = width // half
    part = group // 2
    tile = min(group, 256)
    tiles = group // tile
    emb, hid = w_embed.shape

    features = jnp.asarray(embed_features(length, emb))
    forward = dft_tables(length)

    vmem = pl.BlockSpec(memory_space=pltpu.VMEM)
    dma = pltpu.SemaphoreType.DMA
    dp_steps = len(doubling_steps(dpn))
    members = dpn + chn + n
    each = max(1, tiles // (2 * dpn))
    conv, grad_filter, grad_rate, grad_embed = pl.pallas_call(
        functools.partial(kernel, (n, dpn, chn), tile),
        out_shape=(jax.ShapeDtypeStruct((2, rows, width), NARROW),
                   jax.ShapeDtypeStruct((hid, part), WIDE),
                   jax.ShapeDtypeStruct((8, part), WIDE),
                   jax.ShapeDtypeStruct((emb, hid), WIDE)),
        in_specs=[vmem] * 9,
        out_specs=(pl.BlockSpec(memory_space=pl.ANY), vmem, vmem, vmem),
        scratch_shapes=[
            pltpu.VMEM((hid, part), NARROW),
            pltpu.VMEM((8, part), WIDE),
            pltpu.VMEM((length, hid), NARROW),
            pltpu.VMEM((hid, length), NARROW),
            pltpu.VMEM((length, hid), WIDE),
            pltpu.VMEM((tiles, hid + 16, tile), NARROW),
            pltpu.VMEM((each, 2 * dpn, hid + 16, tile), NARROW),
            pltpu.VMEM((each, hid + 8, tile), WIDE),
            pltpu.VMEM((hid + 8, part), WIDE),
            pltpu.VMEM((2, span, 2 * length), NARROW),
            pltpu.VMEM((2, rows, width), NARROW),
            pltpu.VMEM((2, span, group), NARROW),
            pltpu.VMEM((span, group), NARROW),
            pltpu.VMEM((2, span, group), NARROW),
            pltpu.VMEM((2 * length, group), WIDE),
            pltpu.VMEM((length, group), WIDE),
            pltpu.VMEM((length, group), WIDE),
            pltpu.VMEM((length, tile), NARROW),
            pltpu.VMEM((length, tile), WIDE),
            pltpu.VMEM((length, tile), NARROW),
            pltpu.VMEM((2 * length, tile), WIDE),
            pltpu.VMEM((2 * length, tile), WIDE),
            pltpu.VMEM((2 * length, tile), WIDE),
            pltpu.VMEM((2 * length, tile), NARROW),
            pltpu.VMEM((2 * length, tile), NARROW),
            pltpu.VMEM((2 * length, tile), NARROW),
            pltpu.VMEM((2, hid, part), NARROW),
            pltpu.VMEM((2, 8, part), WIDE),
            pltpu.VMEM((length, hid), WIDE),
            pltpu.VMEM((dp_steps + 1, hid + 8, group), WIDE),
            pltpu.VMEM((dp_steps, hid + 8, group), WIDE),
            pltpu.VMEM((2, hid + 8, part), WIDE),
            pltpu.VMEM((2, hid + 8, part), WIDE),
            pltpu.VMEM((4, emb, hid), WIDE),
            pltpu.VMEM((members, emb, hid), WIDE),
            dma((tiles, half, 3)), dma((tiles, half, 3)),
            dma((tiles, half, 2)), dma((tiles, half, 2)), dma((tiles, 2)),
            dma((dp_steps,)), dma((dp_steps,)),
            dma((members,)), dma((members,)),
            dma((2,)), dma((2,)), dma((2,)), dma((2,)), dma((2,)), dma((2,)),
            dma((tiles,)), dma((each, 2 * dpn)), dma((each, dpn)), dma((each, dpn)),
        ],
        compiler_params=pltpu.CompilerParams(
            collective_id=0, has_side_effects=True, vmem_limit_bytes=60 * 1024 * 1024),
        cost_estimate=pl.CostEstimate(flops=10**10, bytes_accessed=10**7, transcendentals=10**6),
    )(query_input[0], key_input[0], value_input[0], grad_output[0],
      w_embed, features, w_filter, decay_rates[None, :], forward)

    conv_out, conv_grad = conv[0:1].astype(WIDE), conv[1:2].astype(WIDE)
    d_query = (grad_output.astype(WIDE) * conv_out).astype(NARROW)
    d_key = (conv_grad * value_input.astype(WIDE)).astype(NARROW)
    d_value = (conv_grad * key_input.astype(WIDE)).astype(NARROW)
    return (d_query, d_key, d_value, grad_filter, grad_rate[0], grad_embed)


def solution(mesh):
    block = P("dp", "seq", "chan")
    in_specs = (block, block, block, block, P(), P(None, ("chan", "seq")), P(("chan", "seq")))
    out_specs = (block, block, block, P(None, ("chan", "seq")), P(("chan", "seq")), P())
    return jax.shard_map(
        per_device, mesh=mesh, in_specs=in_specs, out_specs=out_specs, check_vma=False
    )
```

```python
import functools
import math

import jax
import jax.numpy as jnp
import numpy as np
from jax import lax
from jax.experimental import pallas as pl
from jax.experimental.pallas import tpu as pltpu
from jax.sharding import PartitionSpec as P

HIGHEST = lax.Precision.HIGHEST
MESH = pl.DeviceIdType.MESH
NARROW = jnp.bfloat16
WIDE = jnp.float32


def embed_features(length, count):
    bands = np.arange(count // 2) + 0.5
    phase = np.arange(length)[None, :] * bands[:, None] * (2.0 * np.pi / length)
    return np.concatenate([np.sin(phase), np.cos(phase)], axis=0).astype(np.float32)


def dft_tables(length):
    turns = np.outer(2 * np.arange(length) + 1, np.arange(length)) % (4 * length)
    angles = turns * (2.0 * np.pi / (4 * length))
    forward = np.concatenate([np.cos(angles), np.sin(angles)], axis=0)
    half = length // 2
    by_half = np.stack([forward[:, :half], forward[:, half:]])
    return by_half.astype(NARROW)


def dot(a, b, dims=((1,), (0,)), precision=None):
    return lax.dot_general(a, b, (dims, ((), ())), preferred_element_type=WIDE, precision=precision)


def doubling_steps(size):
    return [1 << i for i in range(size.bit_length() - 1)]


def flip(index, bit):
    return index + bit - 2 * bit * (lax.rem(lax.div(index, bit), 2))


def kernel(sizes, tile, q_ref, k_ref, v_ref, g_ref, embed_in, feat_ref, filter_in, rate_in, fwd_ref,
           conv_ref, grad_ref, grate_ref, embed_ref,
           filter_ref, rate_ref, hidden_ref, hidden_t_ref, cos_ref, gs_src, gs_got, red_src, fin_all,
           inv_ref, src, a_buf, b_buf, out_buf, h_buf, taps_buf, win_buf, taps_n, corr_buf, weighted_n,
           mine_buf, other_buf, b_spec, join_1, join_2, join_3,
           filter_buf, rate_buf, hg_buf, g_sum, g_got, fin_src, fin_got, e_sum, e_got,
           in_send, in_recv, ret_send, ret_recv, own_sem, red_send, red_recv, emb_send, emb_recv,
           par_send, par_recv, rat_send, rat_recv, fin_send, fin_recv,
           gs_send, gs_recv, all_send, all_recv):
    n, dpn, chn = sizes
    half = n // 2
    rows, width = q_ref.shape
    length = rows * n
    span = rows * half
    group = width // half
    part = group // 2
    tiles = group // tile
    hid = hidden_t_ref.shape[0]
    stream = tiles % (2 * dpn) == 0
    me = lax.axis_index("seq")
    dp = lax.axis_index("dp")
    ch = lax.axis_index("chan")
    up = lax.div(me, half)
    slot = lax.rem(me, half)
    pair = lax.div(me, 2)
    parity = lax.rem(me, 2)

    barrier = pltpu.get_barrier_semaphore()
    greeted = 0
    for o in range(1, n):
        pl.semaphore_signal(barrier, inc=1, device_id=(dp, ch, lax.rem(me + o, n)), device_id_type=MESH)
        greeted += 1
    for o in range(1, dpn):
        for other in ([lax.rem(me + d, n) for d in range(n)] if stream else [me]):
            pl.semaphore_signal(barrier, inc=1, device_id=(lax.rem(dp + o, dpn), ch, other), device_id_type=MESH)
            greeted += 1
    for o in range(1, chn):
        pl.semaphore_signal(barrier, inc=1, device_id=(dp, lax.rem(ch + o, chn), me), device_id_type=MESH)
        greeted += 1
    pl.semaphore_wait(barrier, greeted)

    def col(owner, t):
        return pl.ds(pl.multiple_of(owner * group + t * tile, 128), tile)

    def tcol(t):
        return pl.ds(pl.multiple_of(t * tile, 128), tile)

    def block_rows(i, size, base=0):
        return pl.ds(pl.multiple_of(base + i * size, 16), size)

    my_rows = pl.ds(pl.multiple_of(slot * rows, 16), rows)

    def par_copies(j):
        dest = (dp, ch, pair + j * half)
        return [
            pltpu.make_async_remote_copy(
                src_ref=source, dst_ref=target.at[parity], send_sem=send.at[j],
                recv_sem=recv.at[parity], device_id=dest, device_id_type=MESH)
            for source, target, send, recv in (
                (filter_ref, filter_buf, par_send, par_recv), (rate_ref, rate_buf, rat_send, rat_recv))]

    def par_arrivals(e):
        return [
            pltpu.make_async_remote_copy(
                src_ref=source, dst_ref=target.at[e], send_sem=send.at[0],
                recv_sem=recv.at[e], device_id=(dp, ch, lax.rem(me + 1, n)), device_id_type=MESH)
            for source, target, send, recv in (
                (filter_ref, filter_buf, par_send, par_recv), (rate_ref, rate_buf, rat_send, rat_recv))]

    filter_ref[...] = filter_in[...].astype(NARROW)
    rate_ref[...] = jnp.broadcast_to(rate_in[...], rate_ref.shape)
    for j in (0, 1):
        @pl.when(pair + j * half != me)
        def _():
            for copy in par_copies(j):
                copy.start()

        @pl.when(pair + j * half == me)
        def _():
            filter_buf[parity] = filter_ref[...]
            rate_buf[parity] = rate_ref[...]

    def in_copy(t, o, kind):
        owner = lax.rem(slot + o, half)
        dest = (dp, ch, (up if kind < 2 else 1 - up) * half + owner)
        source = src.at[0 if kind == 0 else 1, :, col(owner, t)]
        if kind == 1:
            target = b_buf.at[my_rows, tcol(t)]
        else:
            target = a_buf.at[up, my_rows, tcol(t)]
        return pltpu.make_async_remote_copy(
            src_ref=source, dst_ref=target, send_sem=in_send.at[t, o, kind],
            recv_sem=in_recv.at[t, o, kind], device_id=dest, device_id_type=MESH)

    def in_kinds(o):
        return (0, 1, 2) if o else (2,)

    def ret_target(t, j):
        return conv_ref.at[1 - up if j == 0 else up, :, col(slot, t)]

    def ret_copy(t, o, j):
        owner = lax.rem(slot + o, half)
        return pltpu.make_async_remote_copy(
            src_ref=out_buf.at[j, pl.ds(pl.multiple_of(owner * rows, 16), rows), tcol(t)],
            dst_ref=ret_target(t, j),
            send_sem=ret_send.at[t, o, j], recv_sem=ret_recv.at[t, o, j],
            device_id=(dp, ch, up * half + owner), device_id_type=MESH)

    def own_copy(t, j):
        return pltpu.make_async_copy(out_buf.at[j, my_rows, tcol(t)], ret_target(t, j), own_sem.at[t, j])

    @pl.loop(0, tiles)
    def _(t):
        for o in list(range(1, half)) + [0]:
            owner = lax.rem(slot + o, half)
            c = col(owner, t)
            p = k_ref[:, c].astype(WIDE) * v_ref[:, c].astype(WIDE)
            u = g_ref[:, c].astype(WIDE) * q_ref[:, c].astype(WIDE)
            src[1 - up, :, c] = p.astype(NARROW)
            src[up, :, c] = u.astype(NARROW)
            for kind in in_kinds(o):
                in_copy(t, o, kind).start()
        c = col(slot, t)
        a_buf[up, my_rows, tcol(t)] = src[0, :, c]
        b_buf[my_rows, tcol(t)] = src[1, :, c]

    each = max(1, tiles // (2 * dpn))

    def gs_dest(t):
        return lax.div(lax.rem(t, tiles // 2), each), ch, 2 * slot + lax.div(t, tiles // 2)

    def gs_place(t):
        return lax.rem(lax.rem(t, tiles // 2), each)

    def gs_copy(t):
        return pltpu.make_async_remote_copy(
            src_ref=gs_src.at[t], dst_ref=gs_got.at[gs_place(t), 2 * dp + up], send_sem=gs_send.at[t],
            recv_sem=gs_recv.at[gs_place(t), 2 * dp + up], device_id=gs_dest(t), device_id_type=MESH)

    def gs_arrival(i, c):
        return pltpu.make_async_remote_copy(
            src_ref=gs_src.at[0], dst_ref=gs_got.at[i, c], send_sem=gs_send.at[0],
            recv_sem=gs_recv.at[i, c], device_id=(dp, ch, lax.rem(me + 1, n)), device_id_type=MESH)

    def all_copy(i, o):
        return pltpu.make_async_remote_copy(
            src_ref=red_src.at[i], dst_ref=fin_all.at[:, tcol(dp * each + i)], send_sem=all_send.at[i, o],
            recv_sem=all_recv.at[i, o], device_id=(lax.rem(dp + o, dpn), ch, me), device_id_type=MESH)

    sign = (2 * up - 1).astype(WIDE)
    scale = 1.0 / (length * math.sqrt(dpn * length))
    time_scale = 1.0 / math.sqrt(length)
    hold = max(0, tiles - 2)
    hg_buf[...] = jnp.zeros_like(hg_buf)
    for i in (0, 1):
        inv_ref[i] = fwd_ref[i].T
    pre_t = dot(embed_in[...], feat_ref[...], ((0,), (0,)), HIGHEST)
    hidden_t = jnp.sin(pre_t)
    hidden_t_ref[...] = hidden_t.astype(NARROW)
    hidden_ref[...] = hidden_t.T.astype(NARROW)
    cos_ref[...] = jnp.cos(pre_t).T
    for e in (0, 1):
        @pl.when(2 * slot + e != me)
        def _():
            for copy in par_arrivals(e):
                copy.wait_recv()

    def pick(ref, t):
        if tile <= part:
            per = part // tile
            return ref[lax.div(t, per), :, tcol(lax.rem(t, per))]
        return jnp.concatenate([ref[0], ref[1]], axis=1)

    step = 32

    def places(i):
        at = lax.broadcasted_iota(jnp.int32, (step, tile), 0) + i * step
        return at.astype(WIDE) * (1.0 / length)

    @pl.loop(0, tiles)
    def _(t):
        tc = tcol(t)
        corr_buf[...] = dot(hidden_ref[...], pick(filter_buf, t))
        rate = pick(rate_buf, t)[0:1]

        @pl.loop(0, length // step)
        def _(i):
            r = block_rows(i, step)
            window = jnp.exp(-rate * places(i))
            taps = corr_buf[r, :] * window
            win_buf[r, tc] = window
            taps_buf[r, tc] = taps
            taps_n[r, :] = (taps * (1.0 / length)).astype(NARROW)

        h_buf[:, tc] = dot(fwd_ref[0], taps_n[:span]) + dot(fwd_ref[1], taps_n[span:])

    @pl.loop(0, tiles)
    def _(t):
        tc = tcol(t)
        for o in range(half):
            for kind in in_kinds(o):
                in_copy(t, o, kind).wait_recv()

        @pl.when(t == hold)
        def _():
            @pl.loop(0, hold)
            def _(early):
                for o in range(1, half):
                    for j in (0, 1):
                        ret_copy(early, o, j).start()

        b_spec[...] = dot(fwd_ref[up], b_buf[:, tc])
        mine_buf[...] = dot(fwd_ref[up], a_buf[up, :, tc])
        other_buf[...] = dot(fwd_ref[1 - up], a_buf[1 - up, :, tc])

        @pl.loop(0, length // step)
        def _(i):
            c, s = block_rows(i, step), block_rows(i, step, length)
            hc, hs = h_buf[c, tc], h_buf[s, tc] * sign
            bc, bs = b_spec[c, :], b_spec[s, :]
            mc, ms = mine_buf[c, :], mine_buf[s, :]
            oc, os = other_buf[c, :], other_buf[s, :]
            ac, as_ = mc + oc, ms + os
            join_1[c, :] = (hc * ac - hs * as_).astype(NARROW)
            join_1[s, :] = (hc * as_ + hs * ac).astype(NARROW)
            join_2[c, :] = (hc * bc + hs * bs).astype(NARROW)
            join_2[s, :] = (hc * bs - hs * bc).astype(NARROW)
            mc, ms = mc + 0.5 * oc, ms + 0.5 * os
            join_3[c, :] = (mc * bc + ms * bs).astype(NARROW)
            join_3[s, :] = ((mc * bs - ms * bc) * sign).astype(NARROW)

        out_buf[0, :, tc] = dot(inv_ref[up], join_1[...]).astype(NARROW)
        out_buf[1, :, tc] = dot(inv_ref[up], join_2[...]).astype(NARROW)
        for j in (0, 1):
            own_copy(t, j).start()

        @pl.when(t >= hold)
        def _():
            for o in range(1, half):
                for j in (0, 1):
                    ret_copy(t, o, j).start()

        for i in (0, 1):
            corr_buf[i * span:(i + 1) * span] = dot(inv_ref[i], join_3[...])

        def finish(i, rate):
            r = block_rows(i, step)
            corr = corr_buf[r, :] * scale
            weighted_n[r, :] = (corr * win_buf[r, tc]).astype(NARROW)
            return rate + jnp.sum(places(i) * taps_buf[r, tc] * corr, axis=0, keepdims=True)

        rate = lax.fori_loop(0, length // step, finish, jnp.zeros((1, tile), WIDE))
        grad = dot(hidden_t_ref[...], weighted_n[...]) * time_scale
        rate = rate * -time_scale
        if stream:
            gs_src[t, 0:hid] = grad.astype(NARROW)
            gs_src[t, hid:hid + 16] = jnp.broadcast_to(rate, (16, tile)).astype(NARROW)
            mine = jnp.logical_and(gs_dest(t)[0] == dp, gs_dest(t)[2] == me)

            @pl.when(jnp.logical_not(mine))
            def _():
                gs_copy(t).start()

            @pl.when(mine)
            def _():
                gs_got[gs_place(t), 2 * dp + up] = gs_src[t]
        else:
            g_sum[0, 0:hid, tc] = grad
            g_sum[0, hid:hid + 8, tc] = jnp.broadcast_to(rate, (8, tile))
        hg_buf[...] += dot(weighted_n[...], pick(filter_buf, t), ((1,), (1,)))

    e_sum[0] = dot(feat_ref[...], hg_buf[...] * cos_ref[...], precision=HIGHEST) * time_scale

    def embed_round(axis, base, size, index, dest):
        def copy(o):
            return pltpu.make_async_remote_copy(
                src_ref=e_sum.at[axis], dst_ref=e_got.at[base + index], send_sem=emb_send.at[base + o],
                recv_sem=emb_recv.at[base + o], device_id=dest(lax.rem(index + o, size)), device_id_type=MESH)

        e_got[base + index] = e_sum[axis]
        for o in range(1, size):
            copy(o).start()
        for o in range(1, size):
            copy(o).wait()
        total = e_got[base]
        for o in range(1, size):
            total = total + e_got[base + o]
        e_sum[axis + 1] = total

    embed_round(0, 0, dpn, dp, lambda at: (at, ch, me))
    embed_round(1, dpn, chn, ch, lambda at: (dp, at, me))

    if stream:
        for i in range(each):
            total = jnp.zeros((hid + 8, tile), WIDE)
            for c in range(2 * dpn):
                mine = jnp.logical_and(dp == c // 2, (c % 2) * half + pair == me)

                @pl.when(jnp.logical_not(mine))
                def _():
                    gs_arrival(i, c).wait_recv()

                total = total + gs_got[i, c].astype(WIDE)[:hid + 8]
            red_src[i] = total
            for o in range(1, dpn):
                all_copy(i, o).start()
            fin_all[:, tcol(dp * each + i)] = total

    i = 0
    for bit in ([] if stream else doubling_steps(dpn)):
        copy = pltpu.make_async_remote_copy(
            src_ref=g_sum.at[i], dst_ref=g_got.at[i], send_sem=red_send.at[i],
            recv_sem=red_recv.at[i], device_id=(flip(dp, bit), ch, me), device_id_type=MESH)
        copy.start()
        copy.wait()
        g_sum[i + 1] = g_sum[i] + g_got[i]
        i += 1

    owners = () if stream else (0, 1)
    for e in owners:
        fin_src[e] = g_sum[i, :, e * part:(e + 1) * part]

    def fin_copy(e):
        return pltpu.make_async_remote_copy(
            src_ref=fin_src.at[e], dst_ref=fin_got.at[up], send_sem=fin_send.at[e],
            recv_sem=fin_recv.at[up], device_id=(dp, ch, 2 * slot + e), device_id_type=MESH)

    def fin_arrival(j):
        return pltpu.make_async_remote_copy(
            src_ref=fin_src.at[0], dst_ref=fin_got.at[j], send_sem=fin_send.at[0],
            recv_sem=fin_recv.at[j], device_id=(dp, ch, lax.rem(me + 1, n)), device_id_type=MESH)

    for e in owners:
        @pl.when(2 * slot + e != me)
        def _():
            fin_copy(e).start()

        @pl.when(2 * slot + e == me)
        def _():
            fin_got[up] = fin_src[e]

    embed_round(2, dpn + chn, n, me, lambda at: (dp, ch, at))
    embed_ref[...] = e_sum[3]

    for j in (0, 1):
        @pl.when(pair + j * half != me)
        def _():
            for copy in par_copies(j):
                copy.wait_send()
    for j in owners:
        @pl.when(pair + j * half != me)
        def _():
            fin_arrival(j).wait_recv()
    for e in owners:
        @pl.when(2 * slot + e != me)
        def _():
            fin_copy(e).wait_send()
    if stream:
        for i in range(each):
            for o in range(1, dpn):
                all_copy(i, o).wait()
    else:
        fin_all[...] = fin_got[0] + fin_got[1]
    grad_ref[...] = fin_all[0:hid]
    grate_ref[...] = fin_all[hid:hid + 8]

    @pl.loop(0, tiles)
    def _(t):
        for o in range(half):
            for j in (0, 1):
                if o:
                    ret_copy(t, o, j).wait()
                else:
                    own_copy(t, j).wait()
            for kind in in_kinds(o):
                in_copy(t, o, kind).wait_send()
        if stream:
            @pl.when(jnp.logical_not(jnp.logical_and(gs_dest(t)[0] == dp, gs_dest(t)[2] == me)))
            def _():
                gs_copy(t).wait_send()


def per_device(query_input, key_input, value_input, grad_output, w_embed, w_filter, decay_rates):
    n, dpn, chn = lax.axis_size("seq"), lax.axis_size("dp"), lax.axis_size("chan")
    rows, width = query_input.shape[1:]
    length = rows * n
    half = n // 2
    span = half * rows
    group = width // half
    part = group // 2
    tile = min(group, 256)
    tiles = group // tile
    emb, hid = w_embed.shape

    features = jnp.asarray(embed_features(length, emb))
    forward = dft_tables(length)

    vmem = pl.BlockSpec(memory_space=pltpu.VMEM)
    dma = pltpu.SemaphoreType.DMA
    dp_steps = len(doubling_steps(dpn))
    members = dpn + chn + n
    each = max(1, tiles // (2 * dpn))
    conv, grad_filter, grad_rate, grad_embed = pl.pallas_call(
        functools.partial(kernel, (n, dpn, chn), tile),
        out_shape=(jax.ShapeDtypeStruct((2, rows, width), NARROW),
                   jax.ShapeDtypeStruct((hid, part), WIDE),
                   jax.ShapeDtypeStruct((8, part), WIDE),
                   jax.ShapeDtypeStruct((emb, hid), WIDE)),
        in_specs=[vmem] * 9,
        out_specs=(pl.BlockSpec(memory_space=pl.ANY), vmem, vmem, vmem),
        scratch_shapes=[
            pltpu.VMEM((hid, part), NARROW),
            pltpu.VMEM((8, part), WIDE),
            pltpu.VMEM((length, hid), NARROW),
            pltpu.VMEM((hid, length), NARROW),
            pltpu.VMEM((length, hid), WIDE),
            pltpu.VMEM((tiles, hid + 16, tile), NARROW),
            pltpu.VMEM((each, 2 * dpn, hid + 16, tile), NARROW),
            pltpu.VMEM((each, hid + 8, tile), WIDE),
            pltpu.VMEM((hid + 8, part), WIDE),
            pltpu.VMEM((2, span, 2 * length), NARROW),
            pltpu.VMEM((2, rows, width), NARROW),
            pltpu.VMEM((2, span, group), NARROW),
            pltpu.VMEM((span, group), NARROW),
            pltpu.VMEM((2, span, group), NARROW),
            pltpu.VMEM((2 * length, group), WIDE),
            pltpu.VMEM((length, group), WIDE),
            pltpu.VMEM((length, group), WIDE),
            pltpu.VMEM((length, tile), NARROW),
            pltpu.VMEM((length, tile), WIDE),
            pltpu.VMEM((length, tile), NARROW),
            pltpu.VMEM((2 * length, tile), WIDE),
            pltpu.VMEM((2 * length, tile), WIDE),
            pltpu.VMEM((2 * length, tile), WIDE),
            pltpu.VMEM((2 * length, tile), NARROW),
            pltpu.VMEM((2 * length, tile), NARROW),
            pltpu.VMEM((2 * length, tile), NARROW),
            pltpu.VMEM((2, hid, part), NARROW),
            pltpu.VMEM((2, 8, part), WIDE),
            pltpu.VMEM((length, hid), WIDE),
            pltpu.VMEM((dp_steps + 1, hid + 8, group), WIDE),
            pltpu.VMEM((dp_steps, hid + 8, group), WIDE),
            pltpu.VMEM((2, hid + 8, part), WIDE),
            pltpu.VMEM((2, hid + 8, part), WIDE),
            pltpu.VMEM((4, emb, hid), WIDE),
            pltpu.VMEM((members, emb, hid), WIDE),
            dma((tiles, half, 3)), dma((tiles, half, 3)),
            dma((tiles, half, 2)), dma((tiles, half, 2)), dma((tiles, 2)),
            dma((dp_steps,)), dma((dp_steps,)),
            dma((members,)), dma((members,)),
            dma((2,)), dma((2,)), dma((2,)), dma((2,)), dma((2,)), dma((2,)),
            dma((tiles,)), dma((each, 2 * dpn)), dma((each, dpn)), dma((each, dpn)),
        ],
        compiler_params=pltpu.CompilerParams(
            collective_id=0, has_side_effects=True, vmem_limit_bytes=60 * 1024 * 1024),
        cost_estimate=pl.CostEstimate(flops=10**10, bytes_accessed=10**7, transcendentals=10**6),
    )(query_input[0], key_input[0], value_input[0], grad_output[0],
      w_embed, features, w_filter, decay_rates[None, :], forward)

    conv_out, conv_grad = conv[0:1].astype(WIDE), conv[1:2].astype(WIDE)
    d_query = (grad_output.astype(WIDE) * conv_out).astype(NARROW)
    d_key = (conv_grad * value_input.astype(WIDE)).astype(NARROW)
    d_value = (conv_grad * key_input.astype(WIDE)).astype(NARROW)
    return (d_query, d_key, d_value, grad_filter, grad_rate[0], grad_embed)


def solution(mesh):
    block = P("dp", "seq", "chan")
    in_specs = (block, block, block, block, P(), P(None, ("chan", "seq")), P(("chan", "seq")))
    out_specs = (block, block, block, P(None, ("chan", "seq")), P(("chan", "seq")), P())
    return jax.shard_map(
        per_device, mesh=mesh, in_specs=in_specs, out_specs=out_specs, check_vma=False
    )
```
